1024 devices in a mesh: ev: 16 (over z), blk: 64 (over y, x, core).
Axes of the slice: x: 4, y: 8, z: 16, core: 2. Of those that a mesh axis runs over, the one named last changes fastest.
Arguments:
- kernel_tiles: bfloat16 [16, 64, 24, 6, 2048], P('ev', 'blk'), may hold values from -6 to 6
- region: int32 [16, 64, 24], P('ev', 'blk'), may hold values from 0 to 63, as said below
- band_width: int32 [8], replicated, may hold values from 2 to 16
Outputs:
- smoothed: float32 [3, 128, 131072], P(None, None, ('ev', 'blk'))
The draws below stay inside these ranges and needn't reach their ends.
Inputs may be any that keep to these rules, and one draw needn't show every extreme that they name: `region`: each device's 24 entries are distinct, and no more than 2 of them lie in one lateral section (numbers s * 4 to s * 4 + 3); every device has 2 in some section.
All inputs are finite; a program needn't handle non-finite values.
Results may differ from the reference program's by a relative error of at most 0.015.
Values may be sent and summed in bfloat16 or wider, within the bound.
No kernel may reach another device: no remote copies, remote signals or barrier semaphores. Data moves between devices by JAX's collectives and lax.ppermute only.
A program may use at most 32 MiB of HBM per device.

```python
import jax
import jax.numpy as jnp
from jax import lax

NT = 4
CAP = 2
LAYERS = 8
ZS = 2
TW = 2048
EVG = 16
BLKS = 64
KB = 24
Z = 128
LAT = 131072


def draw_region(key, part):
    key = jax.random.fold_in(key, 11)
    key_zero, key_rank, key_tile, key_order = jax.random.split(key, 4)
    count = EVG * BLKS
    zeros_n = jax.random.randint(key_zero, (count, 1), 0, EVG // 4 + 1)
    twos_n = EVG // 2 + zeros_n
    ranks = jax.vmap(lambda k: jax.random.permutation(k, EVG))(jax.random.split(key_rank, count))
    counts = jnp.where(ranks < zeros_n, 0, jnp.where(ranks < zeros_n + twos_n, 2, 1))
    tile_keys = jax.random.split(key_tile, count * EVG)
    within = jax.vmap(lambda k: jax.random.permutation(k, NT))(tile_keys).reshape(count, EVG, NT)[:, :, :CAP]
    section = jnp.arange(EVG, dtype=jnp.int32)[None, :, None]
    ids_all = (section * NT + within).reshape(count, EVG * CAP)
    valid = (jnp.arange(CAP, dtype=jnp.int32)[None, None, :] < counts[:, :, None]).reshape(count, EVG * CAP)
    position = jnp.cumsum(valid.astype(jnp.int32), axis=1) - 1
    slots = jnp.arange(KB, dtype=jnp.int32)
    hit = valid[:, :, None] & (position[:, :, None] == slots[None, None, :])
    packed = jnp.sum(jnp.where(hit, ids_all[:, :, None], 0), axis=1)
    order = jax.vmap(lambda k: jax.random.permutation(k, KB))(jax.random.split(key_order, count))
    mixed = jnp.take_along_axis(packed, order, axis=1)
    return mixed.reshape(EVG, BLKS, KB).astype(jnp.int32)


def plant(result, key, low, largest):
    longest = result.shape.index(max(result.shape))
    spots = []
    for shift in (0, 1):
        where = [jax.random.randint(jax.random.fold_in(key, axis), (), 0, length) for axis, length in enumerate(result.shape)]
        where[longest] = (where[longest] + shift) % result.shape[longest]
        spots.append(tuple(where))
    return result.at[spots[0]].set(low).at[spots[1]].set(largest)


def block_scale(own_key, shape, cuts, smallest, largest):
    loudness, own = 1.0, jax.random.fold_in(own_key, 6)
    for dim, shards_of in cuts:
        heights = jnp.exp(jax.random.uniform(jax.random.fold_in(own, dim), (shards_of,), jnp.float32, smallest / len(cuts), largest / len(cuts)))
        loudness = loudness * jnp.repeat(heights, shape[dim] // shards_of).reshape([-1 if axis == dim else 1 for axis in range(len(shape))])
    return loudness


def normal_values(rng, shape, scale, most, cuts=(), kind=jnp.bfloat16):
    drawn = jax.random.normal(rng, shape, jnp.float32) * scale
    if len(cuts) > 0:
        drawn = block_scale(rng, shape, cuts, -0.22, 0.18) * drawn
    return jnp.clip(drawn, min=-most, max=most).astype(kind)


def setup_inputs(seed: int = 0) -> dict:
    arg_keys = jax.random.split(jax.random.key(seed), 4)
    return {
        "kernel_tiles": normal_values(arg_keys[0], (EVG, BLKS, KB, 3 * ZS, TW), 1.0, 6.0, ((0, 16), (1, 64))),
        "region": draw_region(jax.random.fold_in(arg_keys[3], 71), 0),
        "band_width": plant(jax.random.randint(arg_keys[2], (LAYERS,), 2, 17), jax.random.fold_in(arg_keys[2], 1), 2, 16).astype(jnp.int32),
    }


def build_smoother(band_width, depth):
    rows = jnp.arange(depth, dtype=jnp.int32)
    layer = rows // (depth // LAYERS)
    pick = (layer[:, None] == jnp.arange(LAYERS, dtype=jnp.int32)[None, :]).astype(jnp.int32)
    half = jnp.sum(pick * band_width[None, :], axis=1)
    dist = jnp.abs(rows[:, None] - rows[None, :])
    weight = jnp.maximum(half[:, None] + 1 - dist, 0).astype(jnp.float32)
    return (weight / jnp.sum(weight, axis=1, keepdims=True)).astype(jnp.bfloat16)


def reference(kernel_tiles, region, band_width):
    total = EVG * NT
    targets = jnp.arange(total, dtype=jnp.int32)

    def per_slab(b):
        tiles_b = kernel_tiles[:, b].reshape(EVG, KB, 3 * ZS * TW).astype(jnp.float32)
        ids_b = region[:, b]
        onehot = (ids_b[:, :, None] == targets[None, None, :]).astype(jnp.float32)
        summed = jnp.einsum("ekt,ekx->tx", onehot, tiles_b, precision=lax.Precision.HIGHEST)
        slab = summed.reshape(EVG, NT, 3, ZS, TW).transpose(2, 3, 0, 1, 4).reshape(3, ZS, LAT)
        return slab.astype(jnp.bfloat16)

    slabs = lax.map(per_slab, jnp.arange(BLKS, dtype=jnp.int32))
    gradient = slabs.transpose(1, 0, 2, 3).reshape(3, Z, LAT)
    smoother = build_smoother(band_width, Z)
    return jnp.einsum("ij,cjl->cil", smoother.astype(jnp.float32), gradient.astype(jnp.float32), precision=lax.Precision.HIGHEST)
```

```python
import jax
import jax.numpy as jnp
from jax import lax
from jax.experimental import pallas as pl
from jax.experimental.pallas import tpu as pltpu
from jax.sharding import PartitionSpec as P

F32 = jnp.float32
BF16 = jnp.bfloat16
I32 = jnp.int32

GROUPS = 16
NT = 4
KB = 24
COMPS = 3
QUARTERS = 4
LANES = 128
LAYERS = 8
SLABS = 64
DATA_ROWS = 192
MSG_ROWS = 200


def iota(shape, dim):
    return lax.broadcasted_iota(I32, shape, dim)


def pack_kernel(ids_ref, tiles_ref, out_ref):
    ids = ids_ref[...]
    section = lax.shift_right_logical(ids, 2)
    tile = ids & 3
    eye = iota((KB, KB), 0) == iota((KB, KB), 1)
    column = jnp.sum(jnp.where(eye, section, 0), axis=1, keepdims=True)
    earlier = (column == section) & (iota((KB, KB), 0) < iota((KB, KB), 1))
    slot = jnp.sum(earlier.astype(I32), axis=0, keepdims=True)

    cols = iota((KB, 8 * KB), 1)
    part = sum((cols >= KB * m).astype(I32) for m in range(1, 8))
    repeat = (cols - KB * part == iota((KB, 8 * KB), 0)).astype(BF16)
    place = jnp.broadcast_to(section * 16 + slot * 2, (8, KB)).astype(F32).astype(BF16)
    target = jnp.dot(place, repeat, preferred_element_type=F32)[:1].astype(I32)
    part = part[:1]
    target = target + lax.shift_right_logical(part, 1) * 4 + (part & 1)
    picks = (iota((256, 8 * KB), 0) == target).astype(F32).astype(BF16)

    for c in range(COMPS):
        rows = tiles_ref[c * 48 : (c + 1) * 48, :]
        stacked = jnp.concatenate([rows[:, h * 512 : (h + 1) * 512] for h in range(QUARTERS)], axis=0)
        placed = jnp.dot(picks, stacked, preferred_element_type=F32)
        for j in range(4):
            start = c * 64 + j * 16
            block = placed[:, j * LANES : (j + 1) * LANES].reshape(GROUPS, 16, LANES)
            out_ref[:, start : start + 16, :] = block.astype(BF16)

    here = lax.shift_right_logical(iota((128, KB), 0), 3) == section
    held = [
        jnp.sum(jnp.where(here & (slot == q), tile + 1, 0), axis=1, keepdims=True) for q in range(2)
    ]
    lane = iota((128, LANES), 1)
    which = jnp.where((lane & 2) != 0, held[1], held[0])
    row = (which - 1) * 32 + (lax.shift_right_logical(lane, 2) & 3) * 8 + (lane & 1) + 1
    notes = jnp.where(which > 0, row, 0).astype(F32).reshape(GROUPS, 8, LANES)
    out_ref[:, DATA_ROWS:MSG_ROWS, :] = notes.astype(BF16)


def sum_kernel(msg_ref, out_ref):
    notes = msg_ref[:, DATA_ROWS:MSG_ROWS, :].astype(F32)
    source = iota((GROUPS, 8, LANES), 1) * 8 + lax.shift_right_logical(iota((GROUPS, 8, LANES), 2), 4)
    notes = jnp.sum(jnp.where(source == iota((GROUPS, 8, LANES), 0), notes, 0.0), axis=0)
    target = notes.astype(I32) - 1
    target = jnp.concatenate([target[0:1, :], target[1:2, :]], axis=1)
    rows = iota((128, 256), 0)
    acc = None
    for c in range(COMPS):
        adds = ((rows == target + 2 * c) & (target >= 0)).astype(F32).astype(BF16)
        blocks = [
            msg_ref[:, c * 64 + j * 16 : c * 64 + (j + 1) * 16, :].reshape(256, LANES) for j in range(4)
        ]
        part = jnp.dot(adds, jnp.concatenate(blocks, axis=1), preferred_element_type=F32)
        acc = part if acc is None else acc + part
    for j in range(4):
        block = acc[:, j * LANES : (j + 1) * LANES].reshape(16, 8, LANES)
        out_ref[:, j, :, :] = block.astype(BF16)


def smooth_kernel(band_ref, slabs_ref, out_ref):
    depth = 2 * SLABS
    grad = slabs_ref[...].astype(F32).reshape(SLABS * 8, LANES).astype(BF16)
    i = iota((depth, SLABS * 8), 0)
    col = iota((depth, SLABS * 8), 1)
    j = lax.shift_right_logical(col, 3) * 2 + (col & 1)
    band = lax.shift_right_logical(iota((depth, 1), 0), 4)
    half = jnp.zeros((depth, 1), I32)
    for n in range(LAYERS):
        half = jnp.where(band == n, band_ref[n], half)
    weight = jnp.maximum(half + 1 - jnp.abs(i - j), 0).astype(F32)
    for c in range(COMPS):
        mine = jnp.where((col & 6) == 2 * c, weight, 0.0)
        smoother = (mine / jnp.sum(mine, axis=1, keepdims=True)).astype(BF16)
        out_ref[c, :, :] = jnp.dot(smoother, grad, preferred_element_type=F32)


VMEM = pl.BlockSpec(memory_space=pltpu.VMEM)
SMEM = pl.BlockSpec(memory_space=pltpu.SMEM)


def shards(kernel_tiles, region, band_width):
    tiles = kernel_tiles[0, 0].transpose(1, 0, 2).reshape(6 * KB, 2048)
    messages = pl.pallas_call(
        pack_kernel,
        out_shape=jax.ShapeDtypeStruct((GROUPS, MSG_ROWS, LANES), BF16),
        in_specs=[VMEM, VMEM],
        out_specs=VMEM,
        name="pack",
    )(region[0], tiles)
    messages = lax.all_to_all(messages, "ev", 0, 0, tiled=True)
    slabs = pl.pallas_call(
        sum_kernel,
        out_shape=jax.ShapeDtypeStruct((16, 4, 8, LANES), BF16),
        in_specs=[VMEM],
        out_specs=VMEM,
        name="add",
    )(messages)
    slabs = lax.all_to_all(slabs.reshape(SLABS, 8, LANES), "blk", 0, 0, tiled=True)
    return pl.pallas_call(
        smooth_kernel,
        out_shape=jax.ShapeDtypeStruct((COMPS, 2 * SLABS, LANES), F32),
        in_specs=[SMEM, VMEM],
        out_specs=VMEM,
        name="smooth",
    )(band_width, slabs)


def solution(mesh):
    in_specs = (P("ev", "blk", None, None, None), P("ev", "blk", None), P())
    out_specs = P(None, None, ("ev", "blk"))
    return jax.shard_map(shards, mesh=mesh, in_specs=in_specs, out_specs=out_specs, check_vma=False)
```

```python
import jax
import jax.numpy as jnp
from jax import lax
from jax.experimental import pallas as pl
from jax.experimental.pallas import tpu as pltpu
from jax.sharding import PartitionSpec as P

F32 = jnp.float32
BF16 = jnp.bfloat16
I32 = jnp.int32

GROUPS = 16
NT = 4
KB = 24
COMPS = 3
QUARTERS = 4
LANES = 128
LAYERS = 8
SLABS = 64
DATA_ROWS = 192
MSG_ROWS = 200


def iota(shape, dim):
    return lax.broadcasted_iota(I32, shape, dim)


def write_smoother(band_ref, smoother_ref):
    depth = 2 * SLABS
    i = iota((depth, SLABS * 8), 0)
    col = iota((depth, SLABS * 8), 1)
    j = (SLABS - 1 - lax.shift_right_logical(col, 3)) * 2 + (col & 1)
    band = lax.shift_right_logical(iota((depth, LAYERS), 0), 4)
    mine = band == iota((depth, LAYERS), 1)
    half = jnp.sum(jnp.where(mine, band_ref[...], 0), axis=1, keepdims=True)
    weight = jnp.maximum(half + 1 - jnp.abs(i - j), 0).astype(F32)
    total = jnp.sum(weight, axis=1, keepdims=True) * 0.25
    smoother = weight / total
    for c in range(COMPS):
        smoother_ref[c, :, :] = jnp.where((col & 6) == 2 * c, smoother, 0.0).astype(BF16)


def pack_kernel(ids_hbm, band_hbm, tiles_hbm, out_ref, smoother_ref, ids_ref, band_ref, tiles_ref, sems):
    ids_copy = pltpu.make_async_copy(ids_hbm, ids_ref, sems.at[6])
    ids_copy.start()
    band_copy = pltpu.make_async_copy(band_hbm, band_ref, sems.at[7])
    band_copy.start()
    copies = []
    for c in range(COMPS):
        for side in range(2):
            part = (pl.ds(c * 48, 48), pl.ds(side * 1024, 1024))
            copies.append(pltpu.make_async_copy(tiles_hbm.at[part], tiles_ref.at[part], sems.at[2 * c + side]))
            copies[-1].start()
    ids_copy.wait()
    ids = ids_ref[...]
    section = lax.shift_right_logical(ids, 2)
    tile = ids & 3
    eye = iota((KB, KB), 0) == iota((KB, KB), 1)
    column = jnp.sum(jnp.where(eye, section, 0), axis=1, keepdims=True)
    earlier = (column == section) & (iota((KB, KB), 0) < iota((KB, KB), 1))
    slot = jnp.sum(earlier.astype(I32), axis=0, keepdims=True)

    cols = iota((KB, 8 * KB), 1)
    part = sum((cols >= KB * m).astype(I32) for m in range(1, 8))
    repeat = (cols - KB * part == iota((KB, 8 * KB), 0)).astype(BF16)
    place = jnp.broadcast_to(section * 16 + slot * 2, (8, KB)).astype(F32).astype(BF16)
    target = jnp.dot(place, repeat, preferred_element_type=F32)[:1].astype(I32)
    part = part[:1]
    target = target + lax.shift_right_logical(part, 1) * 4 + (part & 1)
    picks = (iota((256, 8 * KB), 0) == target).astype(F32).astype(BF16)

    band_copy.wait()
    write_smoother(band_ref, smoother_ref)

    for c in range(COMPS):
        copies[2 * c].wait()
        copies[2 * c + 1].wait()
        rows = tiles_ref[c * 48 : (c + 1) * 48, :]
        stacked = jnp.concatenate([rows[:, h * 512 : (h + 1) * 512] for h in range(QUARTERS)], axis=0)
        placed = jnp.dot(picks, stacked, preferred_element_type=F32)
        for j in range(4):
            start = c * 64 + j * 16
            block = placed[:, j * LANES : (j + 1) * LANES].reshape(GROUPS, 16, LANES)
            out_ref[:, start : start + 16, :] = block.astype(BF16)

    here = lax.shift_right_logical(iota((128, KB), 0), 3) == section
    held = [
        jnp.sum(jnp.where(here & (slot == q), tile + 1, 0), axis=1, keepdims=True) for q in range(2)
    ]
    lane = iota((128, LANES), 1)
    which = jnp.where((lane & 2) != 0, held[1], held[0])
    row = (NT - which) * 32 + (3 - (lax.shift_right_logical(lane, 2) & 3)) * 8 + (lane & 1) + 1
    notes = jnp.where(which > 0, row, 0).astype(F32).reshape(GROUPS, 8, LANES)
    out_ref[:, DATA_ROWS:MSG_ROWS, :] = notes.astype(BF16)


def sum_kernel(msg_ref, out_ref):
    notes = msg_ref[:, DATA_ROWS:MSG_ROWS, :].astype(F32)
    source = iota((GROUPS, 8, LANES), 1) * 8 + lax.shift_right_logical(iota((GROUPS, 8, LANES), 2), 4)
    notes = jnp.sum(jnp.where(source == iota((GROUPS, 8, LANES), 0), notes, 0.0), axis=0)
    target = notes.astype(I32) - 1
    target = jnp.concatenate([target[0:1, :], target[1:2, :]], axis=1)
    rows = iota((128, 256), 0)
    acc = None
    for c in range(COMPS):
        adds = ((rows == target + 2 * c) & (target >= 0)).astype(F32).astype(BF16)
        blocks = [
            msg_ref[:, c * 64 + j * 16 : c * 64 + (j + 1) * 16, :].reshape(256, LANES) for j in range(4)
        ]
        part = jnp.dot(adds, jnp.concatenate(blocks, axis=1), preferred_element_type=F32)
        acc = part if acc is None else acc + part
    for j in range(4):
        block = acc[:, j * LANES : (j + 1) * LANES].reshape(16, 8, LANES)
        out_ref[:, 3 - j, :, :] = block.astype(BF16)


def smooth_kernel(smoother_ref, slabs_ref, out_hbm, out_ref, sems):
    grad = slabs_ref[...].astype(F32).reshape(SLABS * 8, LANES).astype(BF16)
    copies = []
    for c in range(COMPS):
        out_ref[c, :, :] = jnp.dot(smoother_ref[c], grad, preferred_element_type=F32)
        copies.append(pltpu.make_async_copy(out_ref.at[c], out_hbm.at[c], sems.at[c]))
        copies[c].start()
    for copy in copies:
        copy.wait()


BACKWARDS = [list(range(SLABS - 1, -1, -1))]

VMEM = pl.BlockSpec(memory_space=pltpu.VMEM)
HBM = pl.BlockSpec(memory_space=pltpu.HBM)


def in_hbm(array):
    return pltpu.with_memory_space_constraint(array, pltpu.HBM)


def params(mib):
    return pltpu.CompilerParams(vmem_limit_bytes=mib * 1024 * 1024)


def shards(kernel_tiles, region, band_width):
    tiles = kernel_tiles[0, 0].transpose(1, 0, 2).reshape(6 * KB, 2048)
    messages, smoother = pl.pallas_call(
        pack_kernel,
        out_shape=(
            jax.ShapeDtypeStruct((GROUPS, MSG_ROWS, LANES), BF16),
            jax.ShapeDtypeStruct((COMPS, 2 * SLABS, SLABS * 8), BF16),
        ),
        in_specs=[HBM, HBM, HBM],
        out_specs=(VMEM, VMEM),
        scratch_shapes=[
            pltpu.VMEM((1, KB), I32),
            pltpu.VMEM((1, LAYERS), I32),
            pltpu.VMEM((6 * KB, 2048), BF16),
            pltpu.SemaphoreType.DMA((8,)),
        ],
        compiler_params=params(8),
        name="pack",
    )(in_hbm(region[0]), in_hbm(band_width.reshape(1, LAYERS)), in_hbm(tiles))
    messages = lax.all_to_all(messages, "ev", 0, 0, tiled=True)
    slabs = pl.pallas_call(
        sum_kernel,
        out_shape=jax.ShapeDtypeStruct((16, 4, 8, LANES), BF16),
        in_specs=[VMEM],
        out_specs=VMEM,
        compiler_params=params(8),
        name="add",
    )(messages)
    slabs = lax.all_to_all(slabs.reshape(SLABS, 8, LANES), "blk", 0, 0, tiled=True, axis_index_groups=BACKWARDS)
    return pl.pallas_call(
        smooth_kernel,
        out_shape=jax.ShapeDtypeStruct((COMPS, 2 * SLABS, LANES), F32),
        in_specs=[VMEM, VMEM],
        out_specs=HBM,
        scratch_shapes=[
            pltpu.VMEM((COMPS, 2 * SLABS, LANES), F32),
            pltpu.SemaphoreType.DMA((COMPS,)),
        ],
        compiler_params=params(8),
        name="smooth",
    )(smoother, slabs)


def solution(mesh):
    in_specs = (P("ev", "blk", None, None, None), P("ev", "blk", None), P())
    out_specs = P(None, None, ("ev", "blk"))
    return jax.shard_map(shards, mesh=mesh, in_specs=in_specs, out_specs=out_specs, check_vma=False)
```

```python
import jax
import jax.numpy as jnp
from jax import lax
from jax.experimental import pallas as pl
from jax.experimental.pallas import tpu as pltpu
from jax.sharding import PartitionSpec as P

F32 = jnp.float32
BF16 = jnp.bfloat16
I32 = jnp.int32

GROUPS = 16
NT = 4
KB = 24
COMPS = 3
QUARTERS = 4
LANES = 128
LAYERS = 8
SLABS = 64
SECTION_ORDER = [14, 11, 2, 1, 3, 6, 12, 8, 9, 4, 5, 13, 10, 15, 7, 0]
SLAB_ORDER = sorted(range(SLABS), key=lambda b: (-min(b // 8, 8 - b // 8) - min(b // 2 % 4, 4 - b // 2 % 4), -b))
DATA_ROWS = 192
MSG_ROWS = 200


def iota(shape, dim):
    return lax.broadcasted_iota(I32, shape, dim)


def write_smoother(band_ref, level_ref, smoother_ref):
    depth = 2 * SLABS
    i = iota((depth, SLABS * 8), 0)
    col = iota((depth, SLABS * 8), 1)
    j = level_ref[...]
    band = lax.shift_right_logical(iota((depth, LAYERS), 0), 4)
    mine = band == iota((depth, LAYERS), 1)
    half = jnp.sum(jnp.where(mine, band_ref[...], 0), axis=1, keepdims=True)
    weight = jnp.maximum(half + 1 - jnp.abs(i - j), 0).astype(F32)
    total = jnp.sum(weight, axis=1, keepdims=True) * 0.25
    smoother = weight / total
    for c in range(COMPS):
        smoother_ref[c, :, :] = jnp.where((col & 6) == 2 * c, smoother, 0.0).astype(BF16)


def pack_kernel(
    ids_hbm, band_hbm, level_hbm, tiles_hbm, out_ref, smoother_ref, ids_ref, band_ref, level_ref, tiles_ref, sems
):
    ids_copy = pltpu.make_async_copy(ids_hbm, ids_ref, sems.at[6])
    ids_copy.start()
    band_copy = pltpu.make_async_copy(band_hbm, band_ref, sems.at[7])
    band_copy.start()
    level_copy = pltpu.make_async_copy(level_hbm, level_ref, sems.at[8])
    level_copy.start()
    copies = []
    for c in range(COMPS):
        for side in range(2):
            part = (pl.ds(c * 48, 48), pl.ds(side * 1024, 1024))
            copies.append(pltpu.make_async_copy(tiles_hbm.at[part], tiles_ref.at[part], sems.at[2 * c + side]))
            copies[-1].start()
    ids_copy.wait()
    ids = ids_ref[...]
    section = lax.shift_right_logical(ids, 2)
    section = sum(jnp.where(section == s, n, 0) for n, s in enumerate(SECTION_ORDER))
    tile = ids & 3
    eye = iota((KB, KB), 0) == iota((KB, KB), 1)
    column = jnp.sum(jnp.where(eye, section, 0), axis=1, keepdims=True)
    earlier = (column == section) & (iota((KB, KB), 0) < iota((KB, KB), 1))
    slot = jnp.sum(earlier.astype(I32), axis=0, keepdims=True)

    cols = iota((KB, 8 * KB), 1)
    part = sum((cols >= KB * m).astype(I32) for m in range(1, 8))
    repeat = (cols - KB * part == iota((KB, 8 * KB), 0)).astype(BF16)
    place = jnp.broadcast_to(section * 16 + slot * 2, (8, KB)).astype(F32).astype(BF16)
    target = jnp.dot(place, repeat, preferred_element_type=F32)[:1].astype(I32)
    part = part[:1]
    target = target + lax.shift_right_logical(part, 1) * 4 + (part & 1)
    picks = (iota((256, 8 * KB), 0) == target).astype(F32).astype(BF16)

    band_copy.wait()
    level_copy.wait()
    write_smoother(band_ref, level_ref, smoother_ref)

    for c in range(COMPS):
        copies[2 * c].wait()
        copies[2 * c + 1].wait()
        rows = tiles_ref[c * 48 : (c + 1) * 48, :]
        stacked = jnp.concatenate([rows[:, h * 512 : (h + 1) * 512] for h in range(QUARTERS)], axis=0)
        placed = jnp.dot(picks, stacked, preferred_element_type=F32)
        for j in range(4):
            start = c * 64 + j * 16
            block = placed[:, j * LANES : (j + 1) * LANES].reshape(GROUPS, 16, LANES)
            out_ref[:, start : start + 16, :] = block.astype(BF16)

    here = lax.shift_right_logical(iota((128, KB), 0), 3) == section
    held = [
        jnp.sum(jnp.where(here & (slot == q), tile + 1, 0), axis=1, keepdims=True) for q in range(2)
    ]
    lane = iota((128, LANES), 1)
    which = jnp.where((lane & 2) != 0, held[1], held[0])
    row = (which - 1) * 32 + (lax.shift_right_logical(lane, 2) & 3) * 8 + (lane & 1) + 1
    notes = jnp.where(which > 0, row, 0).astype(F32).reshape(GROUPS, 8, LANES)
    out_ref[:, DATA_ROWS:MSG_ROWS, :] = notes.astype(BF16)


def sum_kernel(msg_ref, out_ref):
    notes = msg_ref[:, DATA_ROWS:MSG_ROWS, :].astype(F32)
    source = iota((GROUPS, 8, LANES), 1) * 8 + lax.shift_right_logical(iota((GROUPS, 8, LANES), 2), 4)
    notes = jnp.sum(jnp.where(source == iota((GROUPS, 8, LANES), 0), notes, 0.0), axis=0)
    target = notes.astype(I32) - 1
    target = jnp.concatenate([target[0:1, :], target[1:2, :]], axis=1)
    rows = iota((128, 256), 0)
    acc = None
    for c in range(COMPS):
        adds = ((rows == target + 2 * c) & (target >= 0)).astype(F32).astype(BF16)
        blocks = [
            msg_ref[:, c * 64 + j * 16 : c * 64 + (j + 1) * 16, :].reshape(256, LANES) for j in range(4)
        ]
        part = jnp.dot(adds, jnp.concatenate(blocks, axis=1), preferred_element_type=F32)
        acc = part if acc is None else acc + part
    for j in range(4):
        block = acc[:, j * LANES : (j + 1) * LANES].reshape(16, 8, LANES)
        for n in range(16):
            out_ref[SLAB_ORDER.index(n * 4 + j), :, :] = block[n].astype(BF16)


def smooth_kernel(smoother_ref, slabs_ref, out_hbm, out_ref, sems):
    grad = slabs_ref[...].astype(F32).reshape(SLABS * 8, LANES).astype(BF16)
    copies = []
    for c in range(COMPS):
        out_ref[c, :, :] = jnp.dot(smoother_ref[c], grad, preferred_element_type=F32)
        copies.append(pltpu.make_async_copy(out_ref.at[c], out_hbm.at[c], sems.at[c]))
        copies[c].start()
    for copy in copies:
        copy.wait()


VMEM = pl.BlockSpec(memory_space=pltpu.VMEM)
HBM = pl.BlockSpec(memory_space=pltpu.HBM)


def in_hbm(array):
    return pltpu.with_memory_space_constraint(array, pltpu.HBM)


def params(mib):
    return pltpu.CompilerParams(vmem_limit_bytes=mib * 1024 * 1024)


def shards(kernel_tiles, region, band_width):
    tiles = kernel_tiles[0, 0].transpose(1, 0, 2).reshape(6 * KB, 2048)
    levels = jnp.asarray([[slab * 2 + r % 2 for slab in SLAB_ORDER for r in range(8)]], I32)
    messages, smoother = pl.pallas_call(
        pack_kernel,
        out_shape=(
            jax.ShapeDtypeStruct((GROUPS, MSG_ROWS, LANES), BF16),
            jax.ShapeDtypeStruct((COMPS, 2 * SLABS, SLABS * 8), BF16),
        ),
        in_specs=[HBM, HBM, HBM, HBM],
        out_specs=(VMEM, VMEM),
        scratch_shapes=[
            pltpu.VMEM((1, KB), I32),
            pltpu.VMEM((1, LAYERS), I32),
            pltpu.VMEM((1, SLABS * 8), I32),
            pltpu.VMEM((6 * KB, 2048), BF16),
            pltpu.SemaphoreType.DMA((9,)),
        ],
        compiler_params=params(8),
        name="pack",
    )(in_hbm(region[0]), in_hbm(band_width.reshape(1, LAYERS)), in_hbm(levels), in_hbm(tiles))
    messages = lax.all_to_all(messages, "ev", 0, 0, tiled=True, axis_index_groups=[SECTION_ORDER])
    slabs = pl.pallas_call(
        sum_kernel,
        out_shape=jax.ShapeDtypeStruct((SLABS, 8, LANES), BF16),
        in_specs=[VMEM],
        out_specs=VMEM,
        compiler_params=params(8),
        name="add",
    )(messages)
    slabs = lax.all_to_all(slabs, "blk", 0, 0, tiled=True, axis_index_groups=[SLAB_ORDER])
    return pl.pallas_call(
        smooth_kernel,
        out_shape=jax.ShapeDtypeStruct((COMPS, 2 * SLABS, LANES), F32),
        in_specs=[VMEM, VMEM],
        out_specs=HBM,
        scratch_shapes=[
            pltpu.VMEM((COMPS, 2 * SLABS, LANES), F32),
            pltpu.SemaphoreType.DMA((COMPS,)),
        ],
        compiler_params=params(8),
        name="smooth",
    )(smoother, slabs)


def solution(mesh):
    in_specs = (P("ev", "blk", None, None, None), P("ev", "blk", None), P())
    out_specs = P(None, None, ("ev", "blk"))
    return jax.shard_map(shards, mesh=mesh, in_specs=in_specs, out_specs=out_specs, check_vma=False)
```

```python
import jax
import jax.numpy as jnp
from jax import lax
from jax.experimental import pallas as pl
from jax.experimental.pallas import tpu as pltpu
from jax.sharding import PartitionSpec as P

F32 = jnp.float32
BF16 = jnp.bfloat16
I32 = jnp.int32

GROUPS = 16
NT = 4
KB = 24
COMPS = 3
QUARTERS = 4
LANES = 128
LAYERS = 8
SLABS = 64
SECTION_ORDER = [13, 3, 12, 1, 11, 6, 15, 10, 14, 5, 4, 9, 8, 2, 7, 0]
FIRST_SLAB = 37
SLAB_ORDER = [(FIRST_SLAB + n) % SLABS for n in range(SLABS)]
DATA_ROWS = 192
MSG_ROWS = 200


def iota(shape, dim):
    return lax.broadcasted_iota(I32, shape, dim)


def write_smoother(band_ref, smoother_ref):
    depth = 2 * SLABS
    i = iota((depth, SLABS * 8), 0)
    col = iota((depth, SLABS * 8), 1)
    j = ((lax.shift_right_logical(col, 3) + FIRST_SLAB) & (SLABS - 1)) * 2 + (col & 1)
    band = lax.shift_right_logical(iota((depth, LAYERS), 0), 4)
    mine = band == iota((depth, LAYERS), 1)
    half = jnp.sum(jnp.where(mine, band_ref[...], 0), axis=1, keepdims=True)
    weight = jnp.maximum(half + 1 - jnp.abs(i - j), 0).astype(F32)
    total = jnp.sum(weight, axis=1, keepdims=True) * 0.25
    smoother = weight / total
    for c in range(COMPS):
        smoother_ref[c, :, :] = jnp.where((col & 6) == 2 * c, smoother, 0.0).astype(BF16)


def pack_kernel(ids_hbm, band_hbm, tiles_hbm, out_ref, smoother_ref, ids_ref, band_ref, tiles_ref, sems):
    ids_copy = pltpu.make_async_copy(ids_hbm, ids_ref, sems.at[6])
    ids_copy.start()
    band_copy = pltpu.make_async_copy(band_hbm, band_ref, sems.at[7])
    band_copy.start()
    copies = []
    for c in range(COMPS):
        for side in range(2):
            part = (pl.ds(c * 48, 48), pl.ds(side * 1024, 1024))
            copies.append(pltpu.make_async_copy(tiles_hbm.at[part], tiles_ref.at[part], sems.at[2 * c + side]))
            copies[-1].start()
    ids_copy.wait()
    ids = ids_ref[...]
    section = lax.shift_right_logical(ids, 2)
    section = sum(jnp.where(section == s, n, 0) for n, s in enumerate(SECTION_ORDER))
    tile = ids & 3
    eye = iota((KB, KB), 0) == iota((KB, KB), 1)
    column = jnp.sum(jnp.where(eye, section, 0), axis=1, keepdims=True)
    earlier = (column == section) & (iota((KB, KB), 0) < iota((KB, KB), 1))
    slot = jnp.sum(earlier.astype(I32), axis=0, keepdims=True)

    cols = iota((KB, 8 * KB), 1)
    part = sum((cols >= KB * m).astype(I32) for m in range(1, 8))
    repeat = (cols - KB * part == iota((KB, 8 * KB), 0)).astype(BF16)
    place = jnp.broadcast_to(section * 16 + slot * 2, (8, KB)).astype(F32).astype(BF16)
    target = jnp.dot(place, repeat, preferred_element_type=F32)[:1].astype(I32)
    part = part[:1]
    target = target + lax.shift_right_logical(part, 1) * 4 + (part & 1)
    picks = (iota((256, 8 * KB), 0) == target).astype(F32).astype(BF16)

    band_copy.wait()
    write_smoother(band_ref, smoother_ref)

    for c in range(COMPS):
        copies[2 * c].wait()
        copies[2 * c + 1].wait()
        rows = tiles_ref[c * 48 : (c + 1) * 48, :]
        stacked = jnp.concatenate([rows[:, h * 512 : (h + 1) * 512] for h in range(QUARTERS)], axis=0)
        placed = jnp.dot(picks, stacked, preferred_element_type=F32)
        for j in range(4):
            start = c * 64 + j * 16
            block = placed[:, j * LANES : (j + 1) * LANES].reshape(GROUPS, 16, LANES)
            out_ref[:, start : start + 16, :] = block.astype(BF16)

    here = lax.shift_right_logical(iota((128, KB), 0), 3) == section
    held = [
        jnp.sum(jnp.where(here & (slot == q), tile + 1, 0), axis=1, keepdims=True) for q in range(2)
    ]
    lane = iota((128, LANES), 1)
    which = jnp.where((lane & 2) != 0, held[1], held[0])
    row = (which - 1) * 32 + (lax.shift_right_logical(lane, 2) & 3) * 8 + (lane & 1) + 1
    notes = jnp.where(which > 0, row, 0).astype(F32).reshape(GROUPS, 8, LANES)
    out_ref[:, DATA_ROWS:MSG_ROWS, :] = notes.astype(BF16)


def sum_kernel(msg_ref, out_ref):
    notes = msg_ref[:, DATA_ROWS:MSG_ROWS, :].astype(F32)
    source = iota((GROUPS, 8, LANES), 1) * 8 + lax.shift_right_logical(iota((GROUPS, 8, LANES), 2), 4)
    notes = jnp.sum(jnp.where(source == iota((GROUPS, 8, LANES), 0), notes, 0.0), axis=0)
    target = notes.astype(I32) - 1
    target = jnp.concatenate([target[0:1, :], target[1:2, :]], axis=1)
    rows = iota((128, 256), 0)
    acc = None
    for c in range(COMPS):
        adds = ((rows == target + 2 * c) & (target >= 0)).astype(F32).astype(BF16)
        blocks = [
            msg_ref[:, c * 64 + j * 16 : c * 64 + (j + 1) * 16, :].reshape(256, LANES) for j in range(4)
        ]
        part = jnp.dot(adds, jnp.concatenate(blocks, axis=1), preferred_element_type=F32)
        acc = part if acc is None else acc + part
    for j in range(4):
        block = acc[:, j * LANES : (j + 1) * LANES].reshape(16, 8, LANES)
        for n in range(16):
            out_ref[SLAB_ORDER.index(n * 4 + j), :, :] = block[n].astype(BF16)


def smooth_kernel(smoother_ref, slabs_ref, out_hbm, out_ref, sems):
    grad = slabs_ref[...].astype(F32).reshape(SLABS * 8, LANES).astype(BF16)
    copies = []
    for c in range(COMPS):
        out_ref[c, :, :] = jnp.dot(smoother_ref[c], grad, preferred_element_type=F32)
        copies.append(pltpu.make_async_copy(out_ref.at[c], out_hbm.at[c], sems.at[c]))
        copies[c].start()
    for copy in copies:
        copy.wait()


VMEM = pl.BlockSpec(memory_space=pltpu.VMEM)
HBM = pl.BlockSpec(memory_space=pltpu.HBM)


def in_hbm(array):
    return pltpu.with_memory_space_constraint(array, pltpu.HBM)


def params(mib):
    return pltpu.CompilerParams(vmem_limit_bytes=mib * 1024 * 1024)


def shards(kernel_tiles, region, band_width):
    tiles = kernel_tiles[0, 0].transpose(1, 0, 2).reshape(6 * KB, 2048)
    messages, smoother = pl.pallas_call(
        pack_kernel,
        out_shape=(
            jax.ShapeDtypeStruct((GROUPS, MSG_ROWS, LANES), BF16),
            jax.ShapeDtypeStruct((COMPS, 2 * SLABS, SLABS * 8), BF16),
        ),
        in_specs=[HBM, HBM, HBM],
        out_specs=(VMEM, VMEM),
        scratch_shapes=[
            pltpu.VMEM((1, KB), I32),
            pltpu.VMEM((1, LAYERS), I32),
            pltpu.VMEM((6 * KB, 2048), BF16),
            pltpu.SemaphoreType.DMA((8,)),
        ],
        compiler_params=params(8),
        name="pack",
    )(in_hbm(region[0]), in_hbm(band_width.reshape(1, LAYERS)), in_hbm(tiles))
    messages = lax.all_to_all(messages, "ev", 0, 0, tiled=True, axis_index_groups=[SECTION_ORDER])
    slabs = pl.pallas_call(
        sum_kernel,
        out_shape=jax.ShapeDtypeStruct((SLABS, 8, LANES), BF16),
        in_specs=[VMEM],
        out_specs=VMEM,
        compiler_params=params(8),
        name="add",
    )(messages)
    slabs = lax.all_to_all(slabs, "blk", 0, 0, tiled=True, axis_index_groups=[SLAB_ORDER])
    return pl.pallas_call(
        smooth_kernel,
        out_shape=jax.ShapeDtypeStruct((COMPS, 2 * SLABS, LANES), F32),
        in_specs=[VMEM, VMEM],
        out_specs=HBM,
        scratch_shapes=[
            pltpu.VMEM((COMPS, 2 * SLABS, LANES), F32),
            pltpu.SemaphoreType.DMA((COMPS,)),
        ],
        compiler_params=params(8),
        name="smooth",
    )(smoother, slabs)


def solution(mesh):
    in_specs = (P("ev", "blk", None, None, None), P("ev", "blk", None), P())
    out_specs = P(None, None, ("ev", "blk"))
    return jax.shard_map(shards, mesh=mesh, in_specs=in_specs, out_specs=out_specs, check_vma=False)
```

```python
import jax
import jax.numpy as jnp
from jax import lax
from jax.experimental import pallas as pl
from jax.experimental.pallas import tpu as pltpu
from jax.sharding import PartitionSpec as P

F32 = jnp.float32
BF16 = jnp.bfloat16
I32 = jnp.int32

GROUPS = 16
NT = 4
KB = 24
COMPS = 3
QUARTERS = 4
LANES = 128
LAYERS = 8
SLABS = 64
SECTION_ORDER = [13, 3, 12, 1, 11, 6, 15, 10, 14, 5, 4, 9, 8, 2, 7, 0]
FIRST_SLAB = 37
LATE = 8
SLAB_ORDER = [(FIRST_SLAB + n) % SLABS for n in range(SLABS)]
DATA_ROWS = 192
MSG_ROWS = 200


def iota(shape, dim):
    return lax.broadcasted_iota(I32, shape, dim)


def write_smoother(band_ref, smoother_ref):
    depth = 2 * SLABS
    i = iota((depth, SLABS * 8), 0)
    col = iota((depth, SLABS * 8), 1)
    j = ((lax.shift_right_logical(col, 3) + FIRST_SLAB) & (SLABS - 1)) * 2 + (col & 1)
    band = lax.shift_right_logical(iota((depth, LAYERS), 0), 4)
    mine = band == iota((depth, LAYERS), 1)
    half = jnp.sum(jnp.where(mine, band_ref[...], 0), axis=1, keepdims=True)
    weight = jnp.maximum(half + 1 - jnp.abs(i - j), 0).astype(F32)
    total = jnp.sum(weight, axis=1, keepdims=True) * 0.25
    smoother = weight / total
    for c in range(COMPS):
        smoother_ref[c, :, :] = jnp.where((col & 6) == 2 * c, smoother, 0.0).astype(BF16)


def pack_kernel(ids_hbm, band_hbm, tiles_hbm, out_ref, smoother_ref, ids_ref, band_ref, tiles_ref, sems):
    ids_copy = pltpu.make_async_copy(ids_hbm, ids_ref, sems.at[6])
    ids_copy.start()
    band_copy = pltpu.make_async_copy(band_hbm, band_ref, sems.at[7])
    band_copy.start()
    copies = []
    for c in range(COMPS):
        for side in range(2):
            part = (pl.ds(c * 48, 48), pl.ds(side * 1024, 1024))
            copies.append(pltpu.make_async_copy(tiles_hbm.at[part], tiles_ref.at[part], sems.at[2 * c + side]))
            copies[-1].start()
    ids_copy.wait()
    ids = ids_ref[...]
    section = lax.shift_right_logical(ids, 2)
    section = sum(jnp.where(section == s, n, 0) for n, s in enumerate(SECTION_ORDER))
    tile = ids & 3
    eye = iota((KB, KB), 0) == iota((KB, KB), 1)
    column = jnp.sum(jnp.where(eye, section, 0), axis=1, keepdims=True)
    earlier = (column == section) & (iota((KB, KB), 0) < iota((KB, KB), 1))
    slot = jnp.sum(earlier.astype(I32), axis=0, keepdims=True)

    cols = iota((KB, 8 * KB), 1)
    part = sum((cols >= KB * m).astype(I32) for m in range(1, 8))
    repeat = (cols - KB * part == iota((KB, 8 * KB), 0)).astype(BF16)
    place = jnp.broadcast_to(section * 16 + slot * 2, (8, KB)).astype(F32).astype(BF16)
    target = jnp.dot(place, repeat, preferred_element_type=F32)[:1].astype(I32)
    part = part[:1]
    target = target + lax.shift_right_logical(part, 1) * 4 + (part & 1)
    picks = (iota((256, 8 * KB), 0) == target).astype(F32).astype(BF16)

    band_copy.wait()

    @pl.when(lax.axis_index("ev") < LATE)
    def _():
        write_smoother(band_ref, smoother_ref)

    for c in range(COMPS):
        copies[2 * c].wait()
        copies[2 * c + 1].wait()
        rows = tiles_ref[c * 48 : (c + 1) * 48, :]
        stacked = jnp.concatenate([rows[:, h * 512 : (h + 1) * 512] for h in range(QUARTERS)], axis=0)
        placed = jnp.dot(picks, stacked, preferred_element_type=F32)
        for j in range(4):
            start = c * 64 + j * 16
            block = placed[:, j * LANES : (j + 1) * LANES].reshape(GROUPS, 16, LANES)
            out_ref[:, start : start + 16, :] = block.astype(BF16)

    here = lax.shift_right_logical(iota((128, KB), 0), 3) == section
    held = [
        jnp.sum(jnp.where(here & (slot == q), tile + 1, 0), axis=1, keepdims=True) for q in range(2)
    ]
    lane = iota((128, LANES), 1)
    which = jnp.where((lane & 2) != 0, held[1], held[0])
    row = (which - 1) * 32 + (lax.shift_right_logical(lane, 2) & 3) * 8 + (lane & 1) + 1
    notes = jnp.where(which > 0, row, 0).astype(F32).reshape(GROUPS, 8, LANES)
    out_ref[:, DATA_ROWS:MSG_ROWS, :] = notes.astype(BF16)


def sum_kernel(msg_ref, out_ref):
    notes = msg_ref[:, DATA_ROWS:MSG_ROWS, :].astype(F32)
    source = iota((GROUPS, 8, LANES), 1) * 8 + lax.shift_right_logical(iota((GROUPS, 8, LANES), 2), 4)
    notes = jnp.sum(jnp.where(source == iota((GROUPS, 8, LANES), 0), notes, 0.0), axis=0)
    target = notes.astype(I32) - 1
    target = jnp.concatenate([target[0:1, :], target[1:2, :]], axis=1)
    rows = iota((128, 256), 0)
    acc = None
    for c in range(COMPS):
        adds = ((rows == target + 2 * c) & (target >= 0)).astype(F32).astype(BF16)
        blocks = [
            msg_ref[:, c * 64 + j * 16 : c * 64 + (j + 1) * 16, :].reshape(256, LANES) for j in range(4)
        ]
        part = jnp.dot(adds, jnp.concatenate(blocks, axis=1), preferred_element_type=F32)
        acc = part if acc is None else acc + part
    for j in range(4):
        block = acc[:, j * LANES : (j + 1) * LANES].reshape(16, 8, LANES)
        for n in range(16):
            out_ref[SLAB_ORDER.index(n * 4 + j), :, :] = block[n].astype(BF16)


def smooth_kernel(band_hbm, smoother_ref, slabs_ref, out_hbm, out_ref, band_ref, own_ref, sems):
    late = lax.axis_index("ev") >= LATE

    def smooth(matrix_ref):
        grad = slabs_ref[...].astype(F32).reshape(SLABS * 8, LANES).astype(BF16)
        copies = []
        for c in range(COMPS):
            out_ref[c, :, :] = jnp.dot(matrix_ref[c], grad, preferred_element_type=F32)
            copies.append(pltpu.make_async_copy(out_ref.at[c], out_hbm.at[c], sems.at[c]))
            copies[c].start()
        for copy in copies:
            copy.wait()

    @pl.when(late)
    def _():
        band_copy = pltpu.make_async_copy(band_hbm, band_ref, sems.at[COMPS])
        band_copy.start()
        band_copy.wait()
        write_smoother(band_ref, own_ref)
        smooth(own_ref)

    @pl.when(jnp.logical_not(late))
    def _():
        smooth(smoother_ref)


VMEM = pl.BlockSpec(memory_space=pltpu.VMEM)
HBM = pl.BlockSpec(memory_space=pltpu.HBM)


def in_hbm(array):
    return pltpu.with_memory_space_constraint(array, pltpu.HBM)


def params(mib):
    return pltpu.CompilerParams(vmem_limit_bytes=mib * 1024 * 1024)


def shards(kernel_tiles, region, band_width):
    tiles = kernel_tiles[0, 0].transpose(1, 0, 2).reshape(6 * KB, 2048)
    messages, smoother = pl.pallas_call(
        pack_kernel,
        out_shape=(
            jax.ShapeDtypeStruct((GROUPS, MSG_ROWS, LANES), BF16),
            jax.ShapeDtypeStruct((COMPS, 2 * SLABS, SLABS * 8), BF16),
        ),
        in_specs=[HBM, HBM, HBM],
        out_specs=(VMEM, VMEM),
        scratch_shapes=[
            pltpu.VMEM((1, KB), I32),
            pltpu.VMEM((1, LAYERS), I32),
            pltpu.VMEM((6 * KB, 2048), BF16),
            pltpu.SemaphoreType.DMA((8,)),
        ],
        compiler_params=params(8),
        name="pack",
    )(in_hbm(region[0]), in_hbm(band_width.reshape(1, LAYERS)), in_hbm(tiles))
    messages = lax.all_to_all(messages, "ev", 0, 0, tiled=True, axis_index_groups=[SECTION_ORDER])
    slabs = pl.pallas_call(
        sum_kernel,
        out_shape=jax.ShapeDtypeStruct((SLABS, 8, LANES), BF16),
        in_specs=[VMEM],
        out_specs=VMEM,
        compiler_params=params(8),
        name="add",
    )(messages)
    slabs = lax.all_to_all(slabs, "blk", 0, 0, tiled=True, axis_index_groups=[SLAB_ORDER])
    return pl.pallas_call(
        smooth_kernel,
        out_shape=jax.ShapeDtypeStruct((COMPS, 2 * SLABS, LANES), F32),
        in_specs=[HBM, VMEM, VMEM],
        out_specs=HBM,
        scratch_shapes=[
            pltpu.VMEM((COMPS, 2 * SLABS, LANES), F32),
            pltpu.VMEM((1, LAYERS), I32),
            pltpu.VMEM((COMPS, 2 * SLABS, SLABS * 8), BF16),
            pltpu.SemaphoreType.DMA((COMPS + 1,)),
        ],
        compiler_params=params(8),
        name="smooth",
    )(in_hbm(band_width.reshape(1, LAYERS)), smoother, slabs)


def solution(mesh):
    in_specs = (P("ev", "blk", None, None, None), P("ev", "blk", None), P())
    out_specs = P(None, None, ("ev", "blk"))
    return jax.shard_map(shards, mesh=mesh, in_specs=in_specs, out_specs=out_specs, check_vma=False)
```

```python
import jax
import jax.numpy as jnp
from jax import lax
from jax.experimental import pallas as pl
from jax.experimental.pallas import tpu as pltpu
from jax.sharding import PartitionSpec as P

F32 = jnp.float32
BF16 = jnp.bfloat16
I32 = jnp.int32

GROUPS = 16
NT = 4
KB = 24
COMPS = 3
QUARTERS = 4
LANES = 128
LAYERS = 8
SLABS = 64
SECTION_ORDER = [13, 3, 12, 1, 11, 6, 15, 10, 14, 5, 4, 9, 8, 2, 7, 0]
FIRST_SLAB = 37
SLAB_ORDER = [(FIRST_SLAB + n) % SLABS for n in range(SLABS)]
DATA_ROWS = 192
MSG_ROWS = 200


def iota(shape, dim):
    return lax.broadcasted_iota(I32, shape, dim)


def write_smoother(band_ref, smoother_ref):
    depth = 2 * SLABS
    i = iota((depth, SLABS * 8), 0)
    col = iota((depth, SLABS * 8), 1)
    j = ((lax.shift_right_logical(col, 3) + FIRST_SLAB) & (SLABS - 1)) * 2 + (col & 1)
    band = lax.shift_right_logical(iota((depth, LAYERS), 0), 4)
    mine = band == iota((depth, LAYERS), 1)
    half = jnp.sum(jnp.where(mine, band_ref[...], 0), axis=1, keepdims=True)
    weight = jnp.maximum(half + 1 - jnp.abs(i - j), 0).astype(F32)
    total = jnp.sum(weight, axis=1, keepdims=True) * 0.25
    smoother = weight / total
    for c in range(COMPS):
        smoother_ref[c, :, :] = jnp.where((col & 6) == 2 * c, smoother, 0.0).astype(BF16)


def pack_kernel(ids_hbm, band_hbm, tiles_hbm, out_ref, smoother_ref, ids_ref, band_ref, tiles_ref, sems):
    ids_copy = pltpu.make_async_copy(ids_hbm, ids_ref, sems.at[6])
    ids_copy.start()
    copies = []
    for c in range(COMPS):
        for side in range(2):
            part = (pl.ds(c * 48, 48), pl.ds(side * 1024, 1024))
            copies.append(pltpu.make_async_copy(tiles_hbm.at[part], tiles_ref.at[part], sems.at[2 * c + side]))
            copies[-1].start()
    band_copy = pltpu.make_async_copy(band_hbm, band_ref, sems.at[7])
    band_copy.start()
    ids_copy.wait()
    ids = ids_ref[...]
    section = lax.shift_right_logical(ids, 2)
    section = sum(jnp.where(section == s, n, 0) for n, s in enumerate(SECTION_ORDER))
    tile = ids & 3
    eye = iota((KB, KB), 0) == iota((KB, KB), 1)
    column = jnp.sum(jnp.where(eye, section, 0), axis=1, keepdims=True)
    earlier = (column == section) & (iota((KB, KB), 0) < iota((KB, KB), 1))
    slot = jnp.sum(earlier.astype(I32), axis=0, keepdims=True)

    cols = iota((KB, 8 * KB), 1)
    part = sum((cols >= KB * m).astype(I32) for m in range(1, 8))
    repeat = (cols - KB * part == iota((KB, 8 * KB), 0)).astype(BF16)
    place = jnp.broadcast_to(section * 16 + slot * 2, (8, KB)).astype(F32).astype(BF16)
    target = jnp.dot(place, repeat, preferred_element_type=F32)[:1].astype(I32)
    part = part[:1]
    target = target + lax.shift_right_logical(part, 1) * 4 + (part & 1)
    picks = (iota((256, 8 * KB), 0) == target).astype(F32).astype(BF16)

    band_copy.wait()
    write_smoother(band_ref, smoother_ref)

    for c in range(COMPS):
        copies[2 * c].wait()
        copies[2 * c + 1].wait()
        rows = tiles_ref[c * 48 : (c + 1) * 48, :]
        stacked = jnp.concatenate([rows[:, h * 512 : (h + 1) * 512] for h in range(QUARTERS)], axis=0)
        placed = jnp.dot(picks, stacked, preferred_element_type=F32)
        for j in range(4):
            start = c * 64 + j * 16
            block = placed[:, j * LANES : (j + 1) * LANES].reshape(GROUPS, 16, LANES)
            out_ref[:, start : start + 16, :] = block.astype(BF16)

    here = lax.shift_right_logical(iota((128, KB), 0), 3) == section
    held = [
        jnp.sum(jnp.where(here & (slot == q), tile + 1, 0), axis=1, keepdims=True) for q in range(2)
    ]
    lane = iota((128, LANES), 1)
    which = jnp.where((lane & 2) != 0, held[1], held[0])
    row = (which - 1) * 32 + (lax.shift_right_logical(lane, 2) & 3) * 8 + (lane & 1) + 1
    notes = jnp.where(which > 0, row, 0).astype(F32).reshape(GROUPS, 8, LANES)
    out_ref[:, DATA_ROWS:MSG_ROWS, :] = notes.astype(BF16)


def sum_kernel(msg_ref, out_ref):
    notes = msg_ref[:, DATA_ROWS:MSG_ROWS, :].astype(F32)
    source = iota((GROUPS, 8, LANES), 1) * 8 + lax.shift_right_logical(iota((GROUPS, 8, LANES), 2), 4)
    notes = jnp.sum(jnp.where(source == iota((GROUPS, 8, LANES), 0), notes, 0.0), axis=0)
    target = notes.astype(I32) - 1
    target = jnp.concatenate([target[0:1, :], target[1:2, :]], axis=1)
    rows = iota((128, 256), 0)
    acc = None
    for c in range(COMPS):
        adds = ((rows == target + 2 * c) & (target >= 0)).astype(F32).astype(BF16)
        blocks = [
            msg_ref[:, c * 64 + j * 16 : c * 64 + (j + 1) * 16, :].reshape(256, LANES) for j in range(4)
        ]
        part = jnp.dot(adds, jnp.concatenate(blocks, axis=1), preferred_element_type=F32)
        acc = part if acc is None else acc + part
    for j in range(4):
        block = acc[:, j * LANES : (j + 1) * LANES].reshape(16, 8, LANES)
        for n in range(16):
            out_ref[SLAB_ORDER.index(n * 4 + j), :, :] = block[n].astype(BF16)


def smooth_kernel(smoother_ref, slabs_ref, out_hbm, out_ref, sems):
    grad = slabs_ref[...].astype(F32).reshape(SLABS * 8, LANES).astype(BF16)
    copies = []
    for c in range(COMPS):
        out_ref[c, :, :] = jnp.dot(smoother_ref[c], grad, preferred_element_type=F32)
        copies.append(pltpu.make_async_copy(out_ref.at[c], out_hbm.at[c], sems.at[c]))
        copies[c].start()
    for copy in copies:
        copy.wait()


VMEM = pl.BlockSpec(memory_space=pltpu.VMEM)
HBM = pl.BlockSpec(memory_space=pltpu.HBM)


def in_hbm(array):
    return pltpu.with_memory_space_constraint(array, pltpu.HBM)


def params(mib):
    return pltpu.CompilerParams(vmem_limit_bytes=mib * 1024 * 1024)


def shards(kernel_tiles, region, band_width):
    tiles = kernel_tiles[0, 0].transpose(1, 0, 2).reshape(6 * KB, 2048)
    messages, smoother = pl.pallas_call(
        pack_kernel,
        out_shape=(
            jax.ShapeDtypeStruct((GROUPS, MSG_ROWS, LANES), BF16),
            jax.ShapeDtypeStruct((COMPS, 2 * SLABS, SLABS * 8), BF16),
        ),
        in_specs=[HBM, HBM, HBM],
        out_specs=(VMEM, VMEM),
        scratch_shapes=[
            pltpu.VMEM((1, KB), I32),
            pltpu.VMEM((1, LAYERS), I32),
            pltpu.VMEM((6 * KB, 2048), BF16),
            pltpu.SemaphoreType.DMA((8,)),
        ],
        compiler_params=params(8),
        name="pack",
    )(in_hbm(region[0]), in_hbm(band_width.reshape(1, LAYERS)), in_hbm(tiles))
    messages = lax.all_to_all(messages, "ev", 0, 0, tiled=True, axis_index_groups=[SECTION_ORDER])
    slabs = pl.pallas_call(
        sum_kernel,
        out_shape=jax.ShapeDtypeStruct((SLABS, 8, LANES), BF16),
        in_specs=[VMEM],
        out_specs=VMEM,
        compiler_params=params(8),
        name="add",
    )(messages)
    slabs = lax.all_to_all(slabs, "blk", 0, 0, tiled=True, axis_index_groups=[SLAB_ORDER])
    return pl.pallas_call(
        smooth_kernel,
        out_shape=jax.ShapeDtypeStruct((COMPS, 2 * SLABS, LANES), F32),
        in_specs=[VMEM, VMEM],
        out_specs=HBM,
        scratch_shapes=[
            pltpu.VMEM((COMPS, 2 * SLABS, LANES), F32),
            pltpu.SemaphoreType.DMA((COMPS,)),
        ],
        compiler_params=params(8),
        name="smooth",
    )(smoother, slabs)


def solution(mesh):
    in_specs = (P("ev", "blk", None, None, None), P("ev", "blk", None), P())
    out_specs = P(None, None, ("ev", "blk"))
    return jax.shard_map(shards, mesh=mesh, in_specs=in_specs, out_specs=out_specs, check_vma=False)
```
